512 devices in a mesh: tok: 64 (over x, y, core), col: 8 (over z).
Axes of the slice: x: 4, y: 8, z: 8, core: 2. Of those that a mesh axis runs over, the one named last changes fastest.
Arguments:
- acts: bfloat16 [65536, 18432], P('tok', 'col'), may hold values from -16 to 16
- basis: bfloat16 [65536, 256], P('tok'), may hold values from -0.0234375 to 0.0234375
Outputs:
- corange: bfloat16 [18432, 256], P('col')
- range_next: bfloat16 [65536, 256], P('tok')
The draws below stay inside these ranges and needn't reach their ends.
All inputs are finite; a program needn't handle non-finite values.
Results may differ from the reference program's by a relative error of at most 0.0046.
Values may be sent and summed in bfloat16 or wider, within the bound.
No kernel may reach another device: no remote copies, remote signals or barrier semaphores. Data moves between devices by JAX's collectives and lax.ppermute only.
A program may use at most 64 MiB of HBM per device.

```python
import math
import jax
import jax.numpy as jnp

N = 18432
K = 256
TOKENS = 65536


def spiked(entries, own_key, source, target, blocks, factor):
    def block_of(axis_at):
        return (jnp.arange(entries.shape[axis_at]) // (entries.shape[axis_at] // blocks)).reshape((-1,) + (1,) * (entries.ndim - 1 - axis_at))

    near = jax.random.permutation(own_key, blocks)[block_of(target)]
    second = (block_of(target) + blocks // 2) % blocks
    return jnp.where((block_of(source) == near) | (block_of(source) == second), factor * entries, entries)


def steps_of(stream_key, extent, cuts, least, largest):
    level, own = 1.0, jax.random.fold_in(stream_key, 6)
    for axis_at, shards_of in cuts:
        heights = jnp.exp(jax.random.uniform(jax.random.fold_in(own, axis_at), (shards_of,), jnp.float32, least / len(cuts), largest / len(cuts)))
        level = level * jnp.repeat(heights, extent[axis_at] // shards_of).reshape([-1 if axis == axis_at else 1 for axis in range(len(extent))])
    return level


def normal_values(key, dims, scale, limit, split=(), dtype=jnp.bfloat16):
    array = scale * jax.random.normal(key, dims, jnp.float32)
    if split:
        array = array * steps_of(key, dims, split, -0.22, 0.18)
    return jnp.clip(array, -limit, limit).astype(dtype)


def bell_draw_with(rng, dims, scale, most, pieces, heavy, kind=jnp.bfloat16):
    values = scale * jax.random.normal(rng, dims, jnp.float32)
    if pieces:
        values = values * steps_of(rng, dims, pieces, -0.22, 0.18)
    return jnp.clip(spiked(values, jax.random.fold_in(rng, 3), *heavy), -most, most).astype(kind)


def setup_inputs(seed: int = 0) -> dict:
    key_list = jax.random.split(jax.random.key(seed), 3)
    return {
        "acts": bell_draw_with(key_list[0], (TOKENS, N), 1.0, 16.0, ((0, 64), (1, 8)), (0, 1, 64, 4.0)),
        "basis": normal_values(key_list[1], (TOKENS, K), TOKENS ** -0.5, 0.0234375, ((0, 64),)),
    }


def reference(acts, basis):
    corange = jnp.dot(acts.T, basis, preferred_element_type=jnp.float32).astype(jnp.bfloat16)
    product = jnp.dot(acts, corange, preferred_element_type=jnp.float32)
    range_next = (product * (1.0 / math.sqrt(N))).astype(jnp.bfloat16)
    return (corange, range_next)
```

```python
import math

import jax
import jax.numpy as jnp
from jax import lax
from jax.sharding import Mesh, PartitionSpec as P

N = 18432
XY = ("x", "y")
SWAP = ((0, 1), (1, 0))


def contract_tokens(block, basis):
    return lax.dot_general(
        block, basis, (((0,), (0,)), ((), ())), preferred_element_type=jnp.float32
    )


def exchange_sum(pieces, axes):
    landed = lax.all_to_all(pieces, axes, 0, 0)
    return jnp.sum(landed.astype(jnp.float32), axis=0)


def share(piece, axes, n):
    return lax.all_to_all(jnp.broadcast_to(piece[None], (n,) + piece.shape), axes, 0, 0)


def on_device(acts, basis):
    rows, cols = acts.shape
    k = basis.shape[1]
    half = k // 2
    core = lax.axis_index("core")
    own = core * half
    other = half - own

    partial_b = contract_tokens(acts, basis)
    to_other = lax.dynamic_slice(partial_b, (0, other), (cols, half)).astype(jnp.bfloat16)
    kept = lax.dynamic_slice(partial_b, (0, own), (cols, half))
    from_other = lax.ppermute(to_other, "core", SWAP)
    chip_sum = (kept + from_other.astype(jnp.float32)).astype(jnp.bfloat16)

    piece = exchange_sum(chip_sum.reshape(32, cols // 32, half), XY).astype(jnp.bfloat16)
    mine = share(piece, XY, 32).reshape(cols, half)
    theirs = lax.ppermute(mine, "core", SWAP)
    first = jnp.where(core == 0, mine, theirs)
    second = jnp.where(core == 0, theirs, mine)
    corange = jnp.concatenate([first, second], axis=1)

    partial_y = jnp.dot(acts, corange, preferred_element_type=jnp.float32).astype(jnp.bfloat16)
    summed = exchange_sum(partial_y.reshape(8, rows // 8, k), "z")
    scaled = (summed * (1.0 / math.sqrt(N))).astype(jnp.bfloat16)
    range_next = share(scaled, "z", 8).reshape(rows, k)
    return (corange, range_next)


def solution(mesh):
    fine = Mesh(mesh.devices.reshape(4, 8, 2, 8), ("x", "y", "core", "z"))
    tok = ("x", "y", "core")
    in_specs = (P(tok, "z"), P(tok, None))
    out_specs = (P("z", None), P(tok, None))
    return jax.shard_map(
        on_device, mesh=fine, in_specs=in_specs, out_specs=out_specs, check_vma=False
    )
```

```python
import math

import jax
import jax.numpy as jnp
import numpy as np
from jax import lax
from jax.sharding import Mesh, PartitionSpec as P

N = 18432
SWAP = ((0, 1), (1, 0))
F32, BF16 = jnp.float32, jnp.bfloat16
AXES = ("x", "y", "core", "z")
SIZES = (4, 8, 2, 8)
IDS = np.arange(512).reshape(SIZES)


def xy_groups():
    order = [((p // 8 + p) % 4, 3 * p % 8) for p in range(32)]
    return [
        [int(IDS[x, y, core, z]) for x, y in order] for core in range(2) for z in range(8)
    ]


def z_groups():
    return [
        [int(IDS[x, y, core, (5 if core else 3) * p % 8]) for p in range(8)]
        for x in range(4)
        for y in range(8)
        for core in range(2)
    ]


def exchange(pieces, groups):
    return lax.all_to_all(pieces, AXES, 0, 0, axis_index_groups=groups)


def exchange_sum(pieces, groups):
    return jnp.sum(exchange(pieces, groups).astype(F32), axis=0)


def share(piece, groups):
    n = len(groups[0])
    return exchange(jnp.broadcast_to(piece[None], (n,) + piece.shape), groups)


def on_device(acts, basis):
    rows, cols = acts.shape
    k = basis.shape[1]
    half = k // 2
    core = lax.axis_index("core").astype(jnp.int32)
    own = core * half
    other = half - own

    product = lax.dot_general(acts, basis, (((0,), (0,)), ((), ())), preferred_element_type=F32)
    to_other = lax.dynamic_slice(product, (0, other), (cols, half)).astype(BF16)
    kept = lax.dynamic_slice(product, (0, own), (cols, half))
    from_other = lax.ppermute(to_other, "core", SWAP)
    chip_sum = (kept + from_other.astype(F32)).astype(BF16)
    piece = exchange_sum(chip_sum.reshape(32, cols // 32, half), xy_groups()).astype(BF16)
    mine = share(piece, xy_groups()).reshape(cols, half)
    theirs = lax.ppermute(mine, "core", SWAP)
    first = jnp.where(core == 0, mine, theirs)
    second = jnp.where(core == 0, theirs, mine)
    corange = jnp.concatenate([first, second], axis=1)

    partial_y = jnp.dot(acts, corange, preferred_element_type=F32).astype(BF16)
    summed = exchange_sum(partial_y.reshape(8, rows // 8, k), z_groups())
    scaled = (summed * (1.0 / math.sqrt(N))).astype(BF16)
    range_next = share(scaled, z_groups()).reshape(rows, k)
    return (corange, range_next)


def solution(mesh):
    fine = Mesh(mesh.devices.reshape(SIZES), AXES)
    tok = ("x", "y", "core")
    in_specs = (P(tok, "z"), P(tok, None))
    out_specs = (P("z", None), P(tok, None))
    return jax.shard_map(
        on_device, mesh=fine, in_specs=in_specs, out_specs=out_specs, check_vma=False
    )
```

```python
import math

import jax
import jax.numpy as jnp
import numpy as np
from jax import lax
from jax.experimental import pallas as pl
from jax.experimental.pallas import tpu as pltpu
from jax.sharding import Mesh, PartitionSpec as P

N = 18432
SWAP = ((0, 1), (1, 0))
F32, BF16 = jnp.float32, jnp.bfloat16
AXES = ("x", "y", "core", "z")
SIZES = (4, 8, 2, 8)
LANES = 128
VMEM_LIMIT = 54 * 1024 * 1024
HOLD_LIMIT = 52 * 1024 * 1024
HOLD_PARTS = 4
IDS = np.arange(512).reshape(SIZES)


def xy_groups():
    order = [((p // 8 + p) % 4, 3 * p % 8) for p in range(32)]
    return [
        [int(IDS[x, y, core, z]) for x, y in order] for core in range(2) for z in range(8)
    ]


def z_groups():
    return [
        [int(IDS[x, y, core, (5 if core else 3) * p % 8]) for p in range(8)]
        for x in range(4)
        for y in range(8)
        for core in range(2)
    ]


def exchange(pieces, groups):
    return lax.all_to_all(pieces, AXES, 0, 0, axis_index_groups=groups)


def exchange_sum(pieces, groups):
    return jnp.sum(exchange(pieces, groups).astype(F32), axis=0)


def share(piece, groups):
    n = len(groups[0])
    return exchange(jnp.broadcast_to(piece[None], (n,) + piece.shape), groups)


def half_product_kernel(start_ref, acts_hbm, basis_hbm, out_ref, block_ref, basis_ref, acts_sem, basis_sem):
    groups, half, lanes = out_ref.shape
    start = pl.multiple_of(start_ref[0], LANES)
    basis_copy = pltpu.make_async_copy(basis_hbm, basis_ref, basis_sem)
    acts_copy = pltpu.make_async_copy(acts_hbm.at[:, pl.ds(start, half)], block_ref, acts_sem)
    basis_copy.start()
    acts_copy.start()
    basis_copy.wait()
    basis = basis_ref[...].T
    acts_copy.wait()
    product = jnp.dot(basis, block_ref[...], preferred_element_type=F32)
    turned = product.astype(out_ref.dtype).T
    for g in range(groups):
        out_ref[g] = turned[:, g * lanes : (g + 1) * lanes]


def half_product(acts, basis, start, dtype):
    rows, cols = acts.shape
    k, half = basis.shape[1], cols // 2
    vmem = pl.BlockSpec(memory_space=pltpu.VMEM)
    hbm = pl.BlockSpec(memory_space=pl.ANY)
    return pl.pallas_call(
        half_product_kernel,
        out_shape=pltpu.VMEM((k // LANES, half, LANES), dtype),
        in_specs=[pl.BlockSpec(memory_space=pltpu.SMEM), hbm, hbm],
        out_specs=vmem,
        scratch_shapes=[
            pltpu.VMEM((rows, half), BF16),
            pltpu.VMEM((rows, k), BF16),
            pltpu.SemaphoreType.DMA,
            pltpu.SemaphoreType.DMA,
        ],
        compiler_params=pltpu.CompilerParams(vmem_limit_bytes=VMEM_LIMIT),
        cost_estimate=pl.CostEstimate(
            flops=2 * rows * half * k,
            bytes_accessed=2 * rows * (half + k),
            transcendentals=0,
        ),
    )(start.reshape(1), acts, basis)


def side_by_side(groups):
    return jnp.concatenate([groups[0], groups[1]], axis=1)


def hold_kernel(acts_hbm, after_hbm, held_ref, sems):
    del after_hbm
    rows = held_ref.shape[0] // HOLD_PARTS
    copies = []
    for i in range(HOLD_PARTS):
        at = pl.ds(i * rows, rows)
        copies.append(pltpu.make_async_copy(acts_hbm.at[at], held_ref.at[at], sems.at[i]))
    for copy in copies:
        copy.start()
    for copy in copies:
        copy.wait()


def hold(acts, after):
    hbm = pl.BlockSpec(memory_space=pl.ANY)
    return pl.pallas_call(
        hold_kernel,
        out_shape=pltpu.VMEM(acts.shape, BF16),
        in_specs=[hbm, hbm],
        out_specs=pl.BlockSpec(memory_space=pltpu.VMEM),
        scratch_shapes=[pltpu.SemaphoreType.DMA((HOLD_PARTS,))],
        compiler_params=pltpu.CompilerParams(vmem_limit_bytes=HOLD_LIMIT),
        cost_estimate=pl.CostEstimate(flops=0, bytes_accessed=4 * acts.size, transcendentals=0),
    )(acts, after)


def on_device(acts, basis):
    rows, cols = acts.shape
    k = basis.shape[1]
    half = cols // 2
    core = lax.axis_index("core").astype(jnp.int32)
    own = core * half
    other = half - own

    to_other = half_product(acts, basis, other, BF16)
    from_other = lax.ppermute(to_other, "core", SWAP)
    kept = half_product(acts, basis, own, F32)
    chip_sum = (kept + from_other.astype(F32)).astype(BF16)
    piece = exchange_sum(chip_sum.reshape(32, cols // 32, LANES), xy_groups()).astype(BF16)
    mine = share(piece, xy_groups()).reshape(2, half, LANES)
    theirs = lax.ppermute(mine, "core", SWAP)
    held = hold(acts, piece)
    first = jnp.where(core == 0, mine, theirs)
    second = jnp.where(core == 0, theirs, mine)
    corange = jnp.concatenate([side_by_side(first), side_by_side(second)], axis=0)

    partial_y = jnp.dot(held, corange, preferred_element_type=F32).astype(BF16)
    summed = exchange_sum(partial_y.reshape(8, rows // 8, k), z_groups())
    scaled = (summed * (1.0 / math.sqrt(N))).astype(BF16)
    range_next = share(scaled, z_groups()).reshape(rows, k)
    return (corange, range_next)


def solution(mesh):
    fine = Mesh(mesh.devices.reshape(SIZES), AXES)
    tok = ("x", "y", "core")
    in_specs = (P(tok, "z"), P(tok, None))
    out_specs = (P("z", None), P(tok, None))
    return jax.shard_map(
        on_device, mesh=fine, in_specs=in_specs, out_specs=out_specs, check_vma=False
    )
```

```python
import math

import jax
import jax.numpy as jnp
import numpy as np
from jax import lax
from jax.experimental import pallas as pl
from jax.experimental.pallas import tpu as pltpu
from jax.sharding import Mesh, PartitionSpec as P

N = 18432
SWAP = ((0, 1), (1, 0))
F32, BF16 = jnp.float32, jnp.bfloat16
AXES = ("x", "y", "core", "z")
SIZES = (4, 8, 2, 8)
LANES = 128
VMEM_LIMIT = 54 * 1024 * 1024
HOLD_LIMIT = 52 * 1024 * 1024
HOLD_PARTS = 4
IDS = np.arange(512).reshape(SIZES)


def xy_groups():
    orders = (
        [(p // 8, 3 * p % 8) for p in range(32)],
        [(-(p // 8) % 4, 5 * p % 8) for p in range(32)],
    )
    return [
        [int(IDS[x, y, core, z]) for x, y in orders[core]] for core in range(2) for z in range(8)
    ]


def z_groups():
    order = (0, 2, 4, 6, 1, 3, 5, 7)
    return [
        [int(IDS[x, y, core, z]) for z in order]
        for x in range(4)
        for y in range(8)
        for core in range(2)
    ]


def exchange(pieces, groups):
    return lax.all_to_all(pieces, AXES, 0, 0, axis_index_groups=groups)


def exchange_sum(pieces, groups):
    return jnp.sum(exchange(pieces, groups).astype(F32), axis=0)


def share(piece, groups):
    n = len(groups[0])
    return exchange(jnp.broadcast_to(piece[None], (n,) + piece.shape), groups)


def half_product_kernel(start_ref, acts_hbm, basis_hbm, out_ref, block_ref, basis_ref, acts_sem, basis_sem):
    groups, half, lanes = out_ref.shape
    start = pl.multiple_of(start_ref[0], LANES)
    basis_copy = pltpu.make_async_copy(basis_hbm, basis_ref, basis_sem)
    acts_copy = pltpu.make_async_copy(acts_hbm.at[:, pl.ds(start, half)], block_ref, acts_sem)
    basis_copy.start()
    acts_copy.start()
    basis_copy.wait()
    basis = basis_ref[...].T
    acts_copy.wait()
    product = jnp.dot(basis, block_ref[...], preferred_element_type=F32)
    turned = product.astype(out_ref.dtype).T
    for g in range(groups):
        out_ref[g] = turned[:, g * lanes : (g + 1) * lanes]


def half_product(acts, basis, start, dtype):
    rows, cols = acts.shape
    k, half = basis.shape[1], cols // 2
    vmem = pl.BlockSpec(memory_space=pltpu.VMEM)
    hbm = pl.BlockSpec(memory_space=pl.ANY)
    return pl.pallas_call(
        half_product_kernel,
        out_shape=pltpu.VMEM((k // LANES, half, LANES), dtype),
        in_specs=[pl.BlockSpec(memory_space=pltpu.SMEM), hbm, hbm],
        out_specs=vmem,
        scratch_shapes=[
            pltpu.VMEM((rows, half), BF16),
            pltpu.VMEM((rows, k), BF16),
            pltpu.SemaphoreType.DMA,
            pltpu.SemaphoreType.DMA,
        ],
        compiler_params=pltpu.CompilerParams(vmem_limit_bytes=VMEM_LIMIT),
        cost_estimate=pl.CostEstimate(
            flops=2 * rows * half * k,
            bytes_accessed=2 * rows * (half + k),
            transcendentals=0,
        ),
    )(start.reshape(1), acts, basis)


def side_by_side(groups):
    return jnp.concatenate([groups[0], groups[1]], axis=1)


def hold_kernel(acts_hbm, after_hbm, held_ref, sems):
    del after_hbm
    rows = held_ref.shape[0] // HOLD_PARTS
    copies = []
    for i in range(HOLD_PARTS):
        at = pl.ds(i * rows, rows)
        copies.append(pltpu.make_async_copy(acts_hbm.at[at], held_ref.at[at], sems.at[i]))
    for copy in copies:
        copy.start()
    for copy in copies:
        copy.wait()


def hold(acts, after):
    hbm = pl.BlockSpec(memory_space=pl.ANY)
    return pl.pallas_call(
        hold_kernel,
        out_shape=pltpu.VMEM(acts.shape, BF16),
        in_specs=[hbm, hbm],
        out_specs=pl.BlockSpec(memory_space=pltpu.VMEM),
        scratch_shapes=[pltpu.SemaphoreType.DMA((HOLD_PARTS,))],
        compiler_params=pltpu.CompilerParams(vmem_limit_bytes=HOLD_LIMIT),
        cost_estimate=pl.CostEstimate(flops=0, bytes_accessed=4 * acts.size, transcendentals=0),
    )(acts, after)


def on_device(acts, basis):
    rows, cols = acts.shape
    k = basis.shape[1]
    half = cols // 2
    core = lax.axis_index("core").astype(jnp.int32)
    own = core * half
    other = half - own

    to_other = half_product(acts, basis, other, BF16)
    from_other = lax.ppermute(to_other, "core", SWAP)
    kept = half_product(acts, basis, own, F32)
    chip_sum = (kept + from_other.astype(F32)).astype(BF16)
    piece = exchange_sum(chip_sum.reshape(32, cols // 32, LANES), xy_groups()).astype(BF16)
    mine = share(piece, xy_groups()).reshape(2, half, LANES)
    theirs = lax.ppermute(mine, "core", SWAP)
    held = hold(acts, piece)
    first = jnp.where(core == 0, mine, theirs)
    second = jnp.where(core == 0, theirs, mine)
    corange = jnp.concatenate([side_by_side(first), side_by_side(second)], axis=0)

    partial_y = jnp.dot(held, corange, preferred_element_type=F32).astype(BF16)
    summed = exchange_sum(partial_y.reshape(8, rows // 8, k), z_groups())
    scaled = (summed * (1.0 / math.sqrt(N))).astype(BF16)
    range_next = share(scaled, z_groups()).reshape(rows, k)
    return (corange, range_next)


def solution(mesh):
    fine = Mesh(mesh.devices.reshape(SIZES), AXES)
    tok = ("x", "y", "core")
    in_specs = (P(tok, "z"), P(tok, None))
    out_specs = (P("z", None), P(tok, None))
    return jax.shard_map(
        on_device, mesh=fine, in_specs=in_specs, out_specs=out_specs, check_vma=False
    )
```

```python
import math

import jax
import jax.numpy as jnp
import numpy as np
from jax import lax
from jax.experimental import pallas as pl
from jax.experimental.pallas import tpu as pltpu
from jax.sharding import Mesh, PartitionSpec as P

N = 18432
SWAP = ((0, 1), (1, 0))
F32, BF16 = jnp.float32, jnp.bfloat16
AXES = ("x", "y", "core", "z")
SIZES = (4, 8, 2, 8)
LANES = 128
VMEM_LIMIT = 54 * 1024 * 1024
HOLD_LIMIT = 52 * 1024 * 1024
HOLD_PARTS = 4
IDS = np.arange(512).reshape(SIZES)


def z_groups():
    order = (0, 2, 4, 6, 1, 3, 5, 7)
    return [
        [int(IDS[x, y, core, z]) for z in order]
        for x in range(4)
        for y in range(8)
        for core in range(2)
    ]


def x_groups():
    return [
        [int(IDS[(3 * x if core else x) % 4, y, core, z]) for x in range(4)]
        for y in range(8)
        for core in range(2)
        for z in range(8)
    ]


def y_groups():
    order = (0, 2, 4, 6, 1, 3, 5, 7)
    return [
        [int(IDS[x, y, core, z]) for y in order] for x in range(4) for core in range(2) for z in range(8)
    ]


def exchange(pieces, groups):
    return lax.all_to_all(pieces, AXES, 0, 0, axis_index_groups=groups)


def exchange_sum(pieces, groups):
    return jnp.sum(exchange(pieces, groups).astype(F32), axis=0)


def share(piece, groups):
    n = len(groups[0])
    return exchange(jnp.broadcast_to(piece[None], (n,) + piece.shape), groups)


def half_product_kernel(start_ref, acts_hbm, basis_hbm, out_ref, block_ref, basis_ref, acts_sem, basis_sem):
    groups, half, lanes = out_ref.shape
    start = pl.multiple_of(start_ref[0], LANES)
    basis_copy = pltpu.make_async_copy(basis_hbm, basis_ref, basis_sem)
    acts_copy = pltpu.make_async_copy(acts_hbm.at[:, pl.ds(start, half)], block_ref, acts_sem)
    basis_copy.start()
    acts_copy.start()
    basis_copy.wait()
    basis = basis_ref[...].T
    acts_copy.wait()
    product = jnp.dot(basis, block_ref[...], preferred_element_type=F32)
    turned = product.astype(out_ref.dtype).T
    for g in range(groups):
        out_ref[g] = turned[:, g * lanes : (g + 1) * lanes]


def half_product(acts, basis, start, dtype):
    rows, cols = acts.shape
    k, half = basis.shape[1], cols // 2
    vmem = pl.BlockSpec(memory_space=pltpu.VMEM)
    hbm = pl.BlockSpec(memory_space=pl.ANY)
    return pl.pallas_call(
        half_product_kernel,
        out_shape=pltpu.VMEM((k // LANES, half, LANES), dtype),
        in_specs=[pl.BlockSpec(memory_space=pltpu.SMEM), hbm, hbm],
        out_specs=vmem,
        scratch_shapes=[
            pltpu.VMEM((rows, half), BF16),
            pltpu.VMEM((rows, k), BF16),
            pltpu.SemaphoreType.DMA,
            pltpu.SemaphoreType.DMA,
        ],
        compiler_params=pltpu.CompilerParams(vmem_limit_bytes=VMEM_LIMIT),
        cost_estimate=pl.CostEstimate(
            flops=2 * rows * half * k,
            bytes_accessed=2 * rows * (half + k),
            transcendentals=0,
        ),
    )(start.reshape(1), acts, basis)


def side_by_side(groups):
    return jnp.concatenate([groups[0], groups[1]], axis=1)


def hold_kernel(acts_hbm, after_hbm, held_ref, sems):
    del after_hbm
    rows = held_ref.shape[0] // HOLD_PARTS
    copies = []
    for i in range(HOLD_PARTS):
        at = pl.ds(i * rows, rows)
        copies.append(pltpu.make_async_copy(acts_hbm.at[at], held_ref.at[at], sems.at[i]))
    for copy in copies:
        copy.start()
    for copy in copies:
        copy.wait()


def hold(acts, after):
    hbm = pl.BlockSpec(memory_space=pl.ANY)
    return pl.pallas_call(
        hold_kernel,
        out_shape=pltpu.VMEM(acts.shape, BF16),
        in_specs=[hbm, hbm],
        out_specs=pl.BlockSpec(memory_space=pltpu.VMEM),
        scratch_shapes=[pltpu.SemaphoreType.DMA((HOLD_PARTS,))],
        compiler_params=pltpu.CompilerParams(vmem_limit_bytes=HOLD_LIMIT),
        cost_estimate=pl.CostEstimate(flops=0, bytes_accessed=4 * acts.size, transcendentals=0),
    )(acts, after)


def on_device(acts, basis):
    rows, cols = acts.shape
    k = basis.shape[1]
    half = cols // 2
    core = lax.axis_index("core").astype(jnp.int32)
    own = core * half
    other = half - own

    to_other = half_product(acts, basis, other, BF16)
    from_other = lax.ppermute(to_other, "core", SWAP)
    kept = half_product(acts, basis, own, F32)
    chip_sum = (kept + from_other.astype(F32)).astype(BF16)
    over_x = exchange_sum(chip_sum.reshape(4, cols // 4, LANES), x_groups()).astype(BF16)
    piece = exchange_sum(over_x.reshape(8, cols // 32, LANES), y_groups()).astype(BF16)
    row = share(piece, y_groups()).reshape(cols // 4, LANES)
    mine = share(row, x_groups()).reshape(2, half, LANES)
    theirs = lax.ppermute(mine, "core", SWAP)
    held = hold(acts, piece)
    first = jnp.where(core == 0, mine, theirs)
    second = jnp.where(core == 0, theirs, mine)
    corange = jnp.concatenate([side_by_side(first), side_by_side(second)], axis=0)

    partial_y = jnp.dot(held, corange, preferred_element_type=F32).astype(BF16)
    summed = exchange_sum(partial_y.reshape(8, rows // 8, k), z_groups())
    scaled = (summed * (1.0 / math.sqrt(N))).astype(BF16)
    range_next = share(scaled, z_groups()).reshape(rows, k)
    return (corange, range_next)


def solution(mesh):
    fine = Mesh(mesh.devices.reshape(SIZES), AXES)
    tok = ("x", "y", "core")
    in_specs = (P(tok, "z"), P(tok, None))
    out_specs = (P("z", None), P(tok, None))
    return jax.shard_map(
        on_device, mesh=fine, in_specs=in_specs, out_specs=out_specs, check_vma=False
    )
```
